32 devices in a mesh: groups: 2 (over y), dom: 4 (over z), sub: 2 (over x), col: 2 (over core).
Axes of the slice: x: 2, y: 2, z: 4, core: 2. Of those that a mesh axis runs over, the one named last changes fastest.
Arguments:
- rhs: float32 [8, 2, 3, 16, 512], P(('groups', 'dom'), 'sub', None, 'col'), parts along dimension 0, may hold values from -200 to 200
- diagonal: float32 [4, 2, 3, 512], P('dom', 'sub'), may hold values from 1 to 3
- lower_vals: float32 [4, 2, 3, 3, 7, 512], P('dom', 'sub'), may hold values from -0.013888889 to 0.013888889
- lower_cols: int32 [4, 2, 7, 512], P('dom', 'sub'), may hold values from 0 to 511, as said below
- face_nodes: int32 [4, 2, 4, 256], P('dom', 'sub'), may hold values from 0 to 511, as said below
- couple: float32 [4, 2, 2, 3, 3, 256], P('dom', 'sub'), may hold values from -0.013888889 to 0.013888889
- face_count: int32 [4, 2, 2], P('dom', 'sub'), may hold values from 64 to 256, as said below
Outputs:
- solution: float32 [8, 2, 3, 16, 512], P(('groups', 'dom'), 'sub', None, 'col'), parts along dimension 0
- residual: float32 [8, 2, 3, 16, 512], P(('groups', 'dom'), 'sub', None, 'col'), parts along dimension 0
The draws below stay inside these ranges and needn't reach their ends.
There are 2 independent parts, one for each index of `groups`. The reference program is written for one: setup_inputs(seed, part) draws one part's arguments, and reference() takes and returns one part's arrays. A program takes and returns all parts, laid end to end along the dimension named above; an argument that names none is the same for every part. Nothing has to cross between parts.
Inputs may be any that keep to these rules, and one draw needn't show every extreme that they name: `lower_cols`: for every partition and slot, the row of 512 entries is a permutation of the local nodes. `face_nodes`: each of the four lists of a partition names 256 different local nodes. `face_count`: some pair of each kind has all 256 slots live.
All inputs are finite; a program needn't handle non-finite values.
Results may differ from the reference program's by a relative error of at most 0.0003.
Values sent between devices are 32-bit elements; how exact they have to be, the bound alone decides.
A program may use at most 128 MiB of HBM per device.

```python
import jax
import jax.numpy as jnp
from jax import lax

NODE = 512
SLOTS = 7
IFACE = 256
COLS = 16
ITERS = 2
N_DOM = 4
N_SUB = 2


def draw_rhs(key, part):
    key = jax.random.fold_in(key, 11)
    first, second = jax.random.split(key, 2)
    shape = (N_DOM, N_SUB, 3, COLS, NODE)
    place = jnp.arange(N_DOM, dtype=jnp.float32)[:, None] * N_SUB + jnp.arange(N_SUB, dtype=jnp.float32)[None, :]
    place = place / max(N_DOM * N_SUB - 1, 1)
    ramp = jnp.exp(jnp.log(3.0) * place)
    base = jnp.clip(jax.random.normal(first, shape, jnp.float32), -6.0, 6.0)
    scales = jnp.exp(jax.random.uniform(second, (COLS,), jnp.float32, jnp.log(0.5), jnp.log(5.0)))
    return base * scales[:, None] * ramp[:, :, None, None, None]


def draw_lower_cols(key, part):
    key = jax.random.fold_in(key, 12)
    keys = jax.random.split(key, N_DOM * N_SUB * SLOTS)
    orders = jax.vmap(lambda single: jax.random.permutation(single, NODE))(keys)
    return orders.astype(jnp.int32).reshape(N_DOM, N_SUB, SLOTS, NODE)


def draw_face_nodes(key, part):
    key = jax.random.fold_in(key, 13)
    keys = jax.random.split(key, N_DOM * N_SUB * 4)
    orders = jax.vmap(lambda single: jax.random.permutation(single, NODE)[:IFACE])(keys)
    return orders.astype(jnp.int32).reshape(N_DOM, N_SUB, 4, IFACE)


def draw_face_count(key, part):
    key = jax.random.fold_in(key, 14)
    first, second = jax.random.split(key)
    counts = jax.random.randint(first, (N_DOM * N_SUB, 2), IFACE // 4, IFACE + 1).astype(jnp.int32)
    chosen = jax.random.randint(second, (2,), 0, N_DOM * N_SUB)
    counts = counts.at[chosen[0], 0].set(IFACE).at[chosen[1], 1].set(IFACE)
    return counts.reshape(N_DOM, N_SUB, 2)


def shard_levels(stream_key, extent, cuts, smallest, high):
    def one(position, parts):
        heights = jax.random.uniform(jax.random.fold_in(jax.random.fold_in(stream_key, 6), position), (parts,), jnp.float32, smallest / len(cuts), high / len(cuts))
        return jnp.repeat(jnp.exp(heights), extent[position] // parts).reshape((-1,) + (1,) * (len(extent) - position - 1))

    gain = one(*cuts[0])
    for cut in cuts[1:]:
        gain = gain * one(*cut)
    return gain


def setup_inputs(seed: int = 0, part: int = 0) -> dict:
    key_of = jax.random.split(jax.random.key(seed), 8)
    own_keys = jax.random.split(jax.random.fold_in(key_of[7], part), 8)
    return {
        "rhs": draw_rhs(jax.random.fold_in(jax.random.fold_in(key_of[7], part), 71), part),
        "diagonal": jnp.clip(1.0 + 2.0 * jax.random.uniform(key_of[1], (N_DOM, N_SUB, 3, NODE), jnp.float32) ** shard_levels(key_of[1], (N_DOM, N_SUB, 3, NODE), ((0, 4), (1, 2)), -0.2, 0.2), 1.0, 3.0),
        "lower_vals": jnp.clip(jax.random.uniform(key_of[2], (N_DOM, N_SUB, 3, 3, SLOTS, NODE), jnp.float32, -0.013888889, 0.013888889) * shard_levels(key_of[2], (N_DOM, N_SUB, 3, 3, SLOTS, NODE), ((0, 4), (1, 2)), -0.4, 0.0), -0.013888889, 0.013888889),
        "lower_cols": draw_lower_cols(jax.random.fold_in(key_of[7], 71), part),
        "face_nodes": draw_face_nodes(jax.random.fold_in(key_of[7], 71), part),
        "couple": jnp.clip(jax.random.uniform(key_of[5], (N_DOM, N_SUB, 2, 3, 3, IFACE), jnp.float32, -0.013888889, 0.013888889) * shard_levels(key_of[5], (N_DOM, N_SUB, 2, 3, 3, IFACE), ((0, 4), (1, 2)), -0.4, 0.0), -0.013888889, 0.013888889),
        "face_count": draw_face_count(jax.random.fold_in(key_of[7], 71), part),
    }


def local_apply(field, diagonal_part, blocks, index):
    highest = lax.Precision.HIGHEST
    result = diagonal_part[:, None, :] * field
    near = field[:, :, index]
    result = result + jnp.einsum('abkn,bckn->acn', blocks, near, precision=highest)
    back = jnp.einsum('abkn,acn->bckn', blocks, field, precision=highest)
    return result.at[:, :, index].add(back)

def shift_forward(values, axis):
    zeros = jnp.zeros_like(lax.slice_in_dim(values, 0, 1, axis=axis))
    kept = lax.slice_in_dim(values, 0, values.shape[axis] - 1, axis=axis)
    return jnp.concatenate([zeros, kept], axis=axis)

def shift_backward(values, axis):
    zeros = jnp.zeros_like(lax.slice_in_dim(values, 0, 1, axis=axis))
    kept = lax.slice_in_dim(values, 1, values.shape[axis], axis=axis)
    return jnp.concatenate([kept, zeros], axis=axis)

def pick_nodes(field, positions):
    return field[:, :, positions]

def add_nodes(result, positions, values):
    return result.at[:, :, positions].add(values)

def cholesky_solve(matrix, right):
    order = matrix.shape[0]
    factor = jnp.zeros_like(matrix)
    for j in range(order):
        pivot = jnp.sqrt(matrix[j, j] - jnp.sum(factor[j, :j] * factor[j, :j]))
        factor = factor.at[j, j].set(pivot)
        if j + 1 < order:
            below = matrix[j + 1:, j] - lax.optimization_barrier(jnp.sum(factor[j + 1:, :j] * factor[j, :j][None, :], axis=1))
            factor = factor.at[j + 1:, j].set(below / pivot)
    middle = []
    for j in range(order):
        value = right[j]
        for k in range(j):
            value = value - factor[j, k] * middle[k]
        middle.append(value / factor[j, j])
    answer = [None] * order
    for j in range(order - 1, -1, -1):
        value = middle[j]
        for k in range(j + 1, order):
            value = value - factor[k, j] * answer[k]
        answer[j] = value / factor[j, j]
    return jnp.stack(answer, axis=0)

def reference(rhs, diagonal, lower_vals, lower_cols, face_nodes, couple, face_count):
    highest = lax.Precision.HIGHEST
    slots = jnp.arange(couple.shape[-1], dtype=jnp.int32)
    live = (slots[None, None, None, :] < face_count[:, :, :, None]).astype(jnp.float32)
    masked = couple * live[:, :, :, None, None, :]
    picker = jax.vmap(jax.vmap(pick_nodes))
    adder = jax.vmap(jax.vmap(add_nodes))
    inner = jax.vmap(local_apply)

    def operate(field):
        result = lax.map(lambda pieces: inner(*pieces), (field, diagonal, lower_vals, lower_cols))
        for axis in (0, 1):
            lows = face_nodes[:, :, 2 * axis]
            highs = face_nodes[:, :, 2 * axis + 1]
            weights = masked[:, :, axis]
            sent = jnp.einsum('xyabk,xyack->xybck', weights, picker(field, highs), precision=highest)
            result = adder(result, lows, shift_forward(sent, axis))
            arrived = shift_backward(picker(field, lows), axis)
            result = adder(result, highs, jnp.einsum('xyabk,xybck->xyack', weights, arrived, precision=highest))
        return result

    def gram(left, right):
        return jnp.einsum('xyacn,xyadn->cd', left, right, precision=highest)

    def mixing(whole, coefficients):
        return jnp.einsum('xyacn,cd->xyadn', whole, coefficients, precision=highest)
    solution = jnp.zeros_like(rhs)
    residual = rhs
    directions = rhs
    norms = gram(residual, residual)
    for iteration in range(ITERS):
        images = operate(directions)
        curvature = gram(directions, images)
        alpha = cholesky_solve(curvature, norms)
        solution = solution + mixing(directions, alpha)
        residual = residual - mixing(images, alpha)
        if iteration + 1 < ITERS:
            fresh = gram(residual, residual)
            beta = cholesky_solve(norms, fresh)
            directions = residual + mixing(directions, beta)
            norms = fresh
    return (solution, residual)
```

```python
import functools

import jax
import jax.numpy as jnp
from jax import lax
from jax.experimental import pallas as pl
from jax.experimental.pallas import tpu as pltpu
from jax.sharding import PartitionSpec as P

MESH = pl.DeviceIdType.MESH
SHIFT = 2.0
HIGHEST = lax.Precision.HIGHEST
F32 = jnp.float32


def dot(left, right, dims, precision=None):
    return lax.dot_general(left, right, (dims, ((), ())), precision=precision, preferred_element_type=F32)


NN = ((1,), (0,))
NT = ((1,), (1,))
TN = ((0,), (0,))


def halves(value):
    high = value.astype(jnp.bfloat16).astype(F32)
    return jnp.concatenate([high, value - high], axis=0).astype(jnp.bfloat16)


def joined(value):
    rows = value.shape[0] // 2
    return value[:rows] + value[rows:]


def eliminate(matrix, right):
    order = matrix.shape[0]
    lanes = right.shape[1]
    row = lax.broadcasted_iota(jnp.int32, (order, lanes), 0)
    columns = [jnp.broadcast_to(matrix[:, j : j + 1], (order, lanes)) for j in range(order)]
    scale = jnp.zeros((order, lanes), F32)
    for k in range(order):
        inverse = 1.0 / columns[k][k : k + 1, :]
        scale = jnp.where(row == k, inverse, scale)
        factor = jnp.where(row == k, 0.0, columns[k] * inverse)
        for j in range(k + 1, order):
            columns[j] = columns[j] - factor * columns[j][k : k + 1, :]
        right = right - factor * right[k : k + 1, :]
    return right * scale


def kernel(
    n_dom, n_sub, n_col,
    rhs_ref, diag_ref, vals_ref, cols_ref, faces_ref, couple_ref, count_ref,
    sol_ref, res_ref,
    pick, basis, out_halo, in_halo, weights, message, stage_dom, stage_rest,
    halo_send, halo_recv, col_send, col_recv, dom_send, dom_recv, rest_send, rest_recv,
):
    dom = lax.axis_index("dom")
    sub = lax.axis_index("sub")
    col = lax.axis_index("col")
    width = rhs_ref.shape[1]
    node = rhs_ref.shape[2]
    slots = cols_ref.shape[0]
    iface = faces_ref.shape[1]
    inner = slots * node
    total = width * n_col
    rest = sub * n_col + col
    n_rest = n_sub * n_col

    barrier = pltpu.get_barrier_semaphore()
    for k in range(1, n_dom):
        pl.semaphore_signal(barrier, inc=1, device_id={"dom": lax.rem(dom + k, n_dom)}, device_id_type=MESH)
    for k in range(1, n_rest):
        peer = lax.rem(rest + k, n_rest)
        pl.semaphore_signal(
            barrier, inc=1, device_id={"sub": lax.div(peer, n_col), "col": lax.rem(peer, n_col)}, device_id_type=MESH
        )

    slab = 32

    def build_faces(i, _):
        rows = pl.ds(pl.multiple_of(i * slab, slab), slab)
        ids = lax.broadcasted_iota(jnp.int32, (slab, iface), 0) + i * slab
        for f in range(4):
            hit = ids == faces_ref[f : f + 1, :]
            pick[rows, inner + f * iface : inner + (f + 1) * iface] = jnp.where(hit, 1.0, 0.0).astype(jnp.bfloat16)
        return 0

    def build_inner(i, _):
        rows = pl.ds(pl.multiple_of(i * slab, slab), slab)
        ids = lax.broadcasted_iota(jnp.int32, (slab, node), 0) + i * slab
        for s in range(slots):
            hit = ids == cols_ref[s : s + 1, :]
            pick[rows, s * node : (s + 1) * node] = jnp.where(hit, 1.0, 0.0).astype(jnp.bfloat16)
        return 0

    lax.fori_loop(0, node // slab, build_faces, 0)
    lane = lax.broadcasted_iota(jnp.int32, (3, iface), 1)
    for t in range(2):
        for a in range(3):
            weights[t, a] = jnp.where(lane < count_ref[t], couple_ref[t, a], 0.0)

    basis[0, col] = rhs_ref[...]
    for t in range(2):
        for it in range(2):

            @pl.when((dom == 0) if t == 0 else (sub == 0))
            def _():
                in_halo[it, 2 * t] = jnp.zeros((3 * width, iface), F32)

            @pl.when((dom == n_dom - 1) if t == 0 else (sub == n_sub - 1))
            def _():
                in_halo[it, 2 * t + 1] = jnp.zeros((3 * width, iface), F32)

    pl.semaphore_wait(barrier, n_dom - 1 + n_rest - 1)

    def col_copy(v):
        return pltpu.make_async_remote_copy(
            src_ref=basis.at[v, col], dst_ref=basis.at[v, col],
            send_sem=col_send.at[v], recv_sem=col_recv.at[v],
            device_id={"col": 1 - col}, device_id_type=MESH,
        )

    def halo_copy(it, slot):
        axis, here = ("dom", dom) if slot < 2 else ("sub", sub)
        step = 1 if slot % 2 == 0 else -1
        return pltpu.make_async_remote_copy(
            src_ref=out_halo.at[it, slot], dst_ref=in_halo.at[it, slot],
            send_sem=halo_send.at[it, slot], recv_sem=halo_recv.at[it, slot],
            device_id={axis: here + step}, device_id_type=MESH,
        )

    def sends(slot):
        here, count = (dom, n_dom) if slot < 2 else (sub, n_sub)
        return here < count - 1 if slot % 2 == 0 else here > 0

    def receives(slot):
        here, count = (dom, n_dom) if slot < 2 else (sub, n_sub)
        return here > 0 if slot % 2 == 0 else here < count - 1

    def part(value, a):
        return value[a * width : (a + 1) * width]

    def mix_up(t, value):
        return jnp.concatenate(
            [sum(weights[t, a, b : b + 1, :] * part(value, a) for a in range(3)) for b in range(3)], axis=0
        )

    def mix_down(t, value):
        return jnp.concatenate(
            [sum(weights[t, a, b : b + 1, :] * part(value, b) for b in range(3)) for a in range(3)], axis=0
        )

    def whole(v, a):
        return jnp.concatenate([basis[v, h, a] for h in range(n_col)], axis=0)

    col_copy(0).start()

    for it in range(2):
        field = [basis[it, col, a] for a in range(3)]
        stacked = halves(jnp.concatenate(field, axis=0))
        for t in range(2):
            low = slice(inner + 2 * t * iface, inner + (2 * t + 1) * iface)
            high = slice(inner + (2 * t + 1) * iface, inner + (2 * t + 2) * iface)
            out_halo[it, 2 * t] = mix_up(t, joined(dot(stacked, pick[:, high], NN)))
            out_halo[it, 2 * t + 1] = joined(dot(stacked, pick[:, low], NN))
            for slot in (2 * t, 2 * t + 1):

                @pl.when(sends(slot))
                def _():
                    halo_copy(it, slot).start()

        if it == 0:
            lax.fori_loop(0, node // slab, build_inner, 0)
        result = [(diag_ref[a : a + 1, :] - SHIFT) * field[a] for a in range(3)]
        returned = jnp.zeros((6 * width, node), F32)
        for s in range(slots):
            span = slice(s * node, (s + 1) * node)
            near = joined(dot(stacked, pick[:, span], NN))
            back = []
            for b in range(3):
                back.append(sum(vals_ref[a, b, s : s + 1, :] * field[a] for a in range(3)))
            returned = returned + dot(halves(jnp.concatenate(back, axis=0)), pick[:, span], NT)
            for a in range(3):
                result[a] = result[a] + sum(vals_ref[a, b, s : s + 1, :] * part(near, b) for b in range(3))

        if it == 1:
            col_copy(0).wait_recv()
            col_copy(1).wait_recv()
            zero = jnp.zeros((total, node), F32)
            gram = jnp.zeros((width, 4 * total), F32)
            for a in range(3):
                r0, v1 = whole(0, a), whole(1, a)
                gram = gram + dot(basis[0, col, a], jnp.concatenate([r0, zero, zero, zero], axis=0), NT, HIGHEST)
                gram = gram + dot(field[a], jnp.concatenate([zero, r0, v1, zero], axis=0), NT, HIGHEST)

        for slot in range(4):

            @pl.when(receives(slot))
            def _():
                halo_copy(it, slot).wait_recv()

        for t in range(2):
            first = inner + 2 * t * iface
            arrived = jnp.concatenate([in_halo[it, 2 * t], mix_down(t, in_halo[it, 2 * t + 1])], axis=1)
            returned = returned + dot(halves(arrived), pick[:, first : first + 2 * iface], NT)
        returned = joined(returned)
        for a in range(3):
            result[a] = result[a] + part(returned, a)
            basis[it + 1, col, a] = result[a]
        col_copy(it + 1).start()

    for a in range(3):
        gram = gram + dot(result[a], jnp.concatenate([zero, zero, zero, whole(1, a)], axis=0), NT, HIGHEST)
    message[0] = jnp.concatenate([gram, jnp.zeros((width, 128 - 4 * total), F32)], axis=1)

    def dom_copy(k):
        return pltpu.make_async_remote_copy(
            src_ref=message.at[0], dst_ref=stage_dom.at[dom],
            send_sem=dom_send.at[k], recv_sem=dom_recv.at[k],
            device_id={"dom": lax.rem(dom + k, n_dom)}, device_id_type=MESH,
        )

    def rest_copy(k):
        peer = lax.rem(rest + k, n_rest)
        return pltpu.make_async_remote_copy(
            src_ref=message.at[1], dst_ref=stage_rest.at[rest],
            send_sem=rest_send.at[k], recv_sem=rest_recv.at[k],
            device_id={"sub": lax.div(peer, n_col), "col": lax.rem(peer, n_col)}, device_id_type=MESH,
        )

    for k in range(1, n_dom):
        dom_copy(k).start()
    stage_dom[dom] = message[0]
    for k in range(1, n_dom):
        dom_copy(k).wait_recv()
    message[1] = sum(stage_dom[i] for i in range(n_dom))
    for k in range(1, n_rest):
        rest_copy(k).start()
    stage_rest[rest] = message[1]
    for k in range(1, n_rest):
        rest_copy(k).wait_recv()
    grams = jnp.concatenate(
        [sum(stage_rest[s * n_col + h] for s in range(n_sub)) for h in range(n_col)], axis=0
    )

    s0 = grams[:, : 2 * total]
    s1 = grams[:, total : 3 * total]
    s2 = grams[:, 2 * total : 4 * total]
    norms = s0[:, :total]
    curvature = s1[:, :total] + SHIFT * norms
    big = jnp.concatenate([s0, s1], axis=0)
    stiff = SHIFT * big + jnp.concatenate([s1, s2], axis=0)
    eye = jnp.where(
        lax.broadcasted_iota(jnp.int32, (total, total), 0) == lax.broadcasted_iota(jnp.int32, (total, total), 1), 1.0, 0.0
    )
    alpha0 = eliminate(curvature, norms)
    norms_inverse = eliminate(norms, eye)
    start = eye - SHIFT * alpha0
    mixed = jnp.concatenate([start, -alpha0], axis=0)
    fresh = dot(mixed, dot(big, mixed, NN, HIGHEST), TN, HIGHEST)
    beta = dot(norms_inverse, fresh, NN, HIGHEST)
    direction = jnp.concatenate([start + beta, -alpha0], axis=0)
    curvature = dot(direction, dot(stiff, direction, NN, HIGHEST), TN, HIGHEST)
    alpha1 = eliminate(curvature, fresh)
    moved = dot(direction, alpha1, NN, HIGHEST)
    p_move, q_move = moved[:total], moved[total:]
    nothing = jnp.zeros((total, total), F32)
    sol_mix = jnp.concatenate([alpha0 + p_move, q_move, nothing], axis=0)
    res_mix = jnp.concatenate([start - SHIFT * p_move, -alpha0 - p_move - SHIFT * q_move, -q_move], axis=0)
    both = jnp.concatenate([sol_mix, res_mix], axis=1)

    col_copy(2).wait_recv()
    for a in range(3):
        every = jnp.concatenate([whole(0, a), whole(1, a), whole(2, a)], axis=0)
        answer = dot(both, every, TN, HIGHEST)
        sol_ref[a] = jnp.where(col == 0, answer[:width], answer[width:total])
        res_ref[a] = jnp.where(col == 0, answer[total : total + width], answer[total + width :])

    for v in range(3):
        col_copy(v).wait_send()
    for it in range(2):
        for slot in range(4):

            @pl.when(sends(slot))
            def _():
                halo_copy(it, slot).wait_send()

    for k in range(1, n_dom):
        dom_copy(k).wait_send()
    for k in range(1, n_rest):
        rest_copy(k).wait_send()


def body(n_dom, n_sub, n_col, rhs, diagonal, lower_vals, lower_cols, face_nodes, couple, face_count):
    shape = rhs.shape[2:]
    _, width, node = shape
    slots = lower_cols.shape[2]
    iface = face_nodes.shape[3]
    vmem = pl.BlockSpec(memory_space=pltpu.VMEM)
    dma = pltpu.SemaphoreType.DMA
    sol, res = pl.pallas_call(
        functools.partial(kernel, n_dom, n_sub, n_col),
        out_shape=[jax.ShapeDtypeStruct(shape, F32)] * 2,
        in_specs=[vmem] * 6 + [pl.BlockSpec(memory_space=pltpu.SMEM)],
        out_specs=[vmem] * 2,
        scratch_shapes=[
            pltpu.VMEM((node, slots * node + 4 * iface), jnp.bfloat16),
            pltpu.VMEM((3, n_col, 3, width, node), F32),
            pltpu.VMEM((2, 4, 3 * width, iface), F32),
            pltpu.VMEM((2, 4, 3 * width, iface), F32),
            pltpu.VMEM((2, 3, 3, iface), F32),
            pltpu.VMEM((2, width, 128), F32),
            pltpu.VMEM((n_dom, width, 128), F32),
            pltpu.VMEM((n_sub * n_col, width, 128), F32),
            dma((2, 4)),
            dma((2, 4)),
            dma((3,)),
            dma((3,)),
            dma((n_dom,)),
            dma((n_dom,)),
            dma((n_sub * n_col,)),
            dma((n_sub * n_col,)),
        ],
        compiler_params=pltpu.CompilerParams(
            collective_id=0, has_side_effects=True, vmem_limit_bytes=48 * 1024 * 1024
        ),
    )(rhs[0, 0], diagonal[0, 0], lower_vals[0, 0], lower_cols[0, 0], face_nodes[0, 0], couple[0, 0], face_count[0, 0])
    return sol[None, None], res[None, None]


def solution(mesh):
    field = P(("groups", "dom"), "sub", None, "col", None)
    placed = (
        field,
        P("dom", "sub", None, None),
        P("dom", "sub", None, None, None, None),
        P("dom", "sub", None, None),
        P("dom", "sub", None, None),
        P("dom", "sub", None, None, None, None),
        P("dom", "sub", None),
    )
    return jax.shard_map(
        functools.partial(body, mesh.shape["dom"], mesh.shape["sub"], mesh.shape["col"]),
        mesh=mesh,
        in_specs=placed,
        out_specs=(field, field),
        check_vma=False,
    )
```

```python
import functools

import jax
import jax.numpy as jnp
from jax import lax
from jax.experimental import pallas as pl
from jax.experimental.pallas import tpu as pltpu
from jax.sharding import PartitionSpec as P

MESH = pl.DeviceIdType.MESH
SHIFT = 2.0
HIGHEST = lax.Precision.HIGHEST
F32 = jnp.float32


def dot(left, right, dims, precision=None):
    return lax.dot_general(left, right, (dims, ((), ())), precision=precision, preferred_element_type=F32)


NN = ((1,), (0,))
NT = ((1,), (1,))
TN = ((0,), (0,))


def halves(value):
    high = value.astype(jnp.bfloat16).astype(F32)
    return jnp.concatenate([high, value - high], axis=0).astype(jnp.bfloat16)


def joined(value):
    rows = value.shape[0] // 2
    return value[:rows] + value[rows:]


def eliminate(matrix, right):
    order = matrix.shape[0]
    lanes = right.shape[1]
    row = lax.broadcasted_iota(jnp.int32, (order, lanes), 0)
    columns = [jnp.broadcast_to(matrix[:, j : j + 1], (order, lanes)) for j in range(order)]
    scale = jnp.zeros((order, lanes), F32)
    for k in range(order):
        inverse = 1.0 / columns[k][k : k + 1, :]
        scale = jnp.where(row == k, inverse, scale)
        factor = jnp.where(row == k, 0.0, columns[k] * inverse)
        for j in range(k + 1, order):
            columns[j] = columns[j] - factor * columns[j][k : k + 1, :]
        right = right - factor * right[k : k + 1, :]
    return right * scale


def kernel(
    n_dom, n_sub, n_col,
    rhs_hbm, diag_hbm, vals_hbm, cols_hbm, faces_hbm, couple_hbm, count_hbm,
    out_ref,
    diag_ref, vals_ref, cols_ref, faces_ref, couple_ref, count_ref, load_sem,
    pick, basis, out_halo, in_halo, weights, message, stage,
    halo_send, halo_recv, col_send, col_recv, gram_send, gram_recv,
):
    dom = lax.axis_index("dom")
    sub = lax.axis_index("sub")
    col = lax.axis_index("col")
    width = rhs_hbm.shape[1]
    node = rhs_hbm.shape[2]
    slots = cols_hbm.shape[0]
    iface = faces_hbm.shape[1]
    inner = slots * node
    total = width * n_col
    n_all = n_dom * n_sub * n_col
    me = (dom * n_sub + sub) * n_col + col

    def place(k):
        peer = lax.rem(me + k, n_all)
        return {
            "dom": lax.div(peer, n_sub * n_col),
            "sub": lax.rem(lax.div(peer, n_col), n_sub),
            "col": lax.rem(peer, n_col),
        }

    def every_peer(act):
        if n_all <= 32:
            for k in range(1, n_all):
                act(k)
        else:
            lax.fori_loop(1, n_all, lambda k, _: (act(k), 0)[1], 0)

    def gram_copy(k):
        return pltpu.make_async_remote_copy(
            src_ref=message, dst_ref=stage.at[me], send_sem=gram_send.at[k], recv_sem=gram_recv.at[k],
            device_id=place(k), device_id_type=MESH,
        )

    barrier = pltpu.get_barrier_semaphore()
    every_peer(lambda k: pl.semaphore_signal(barrier, inc=1, device_id=place(k), device_id_type=MESH))

    loads = [
        pltpu.make_async_copy(source, target, load_sem.at[i])
        for i, (source, target) in enumerate(
            [
                (faces_hbm, faces_ref), (rhs_hbm, basis.at[0, col]), (couple_hbm, couple_ref), (count_hbm, count_ref),
                (cols_hbm, cols_ref), (vals_hbm, vals_ref), (diag_hbm, diag_ref),
            ]
        )
    ]
    for load in loads:
        load.start()

    slab = 32

    def build_faces(i, _):
        rows = pl.ds(pl.multiple_of(i * slab, slab), slab)
        ids = lax.broadcasted_iota(jnp.int32, (slab, iface), 0) + i * slab
        for f in range(4):
            hit = ids == faces_ref[f : f + 1, :]
            pick[rows, inner + f * iface : inner + (f + 1) * iface] = jnp.where(hit, 1.0, 0.0).astype(jnp.bfloat16)
        return 0

    def build_inner(i, _):
        rows = pl.ds(pl.multiple_of(i * slab, slab), slab)
        ids = lax.broadcasted_iota(jnp.int32, (slab, node), 0) + i * slab
        for s in range(slots):
            hit = ids == cols_ref[s]
            pick[rows, s * node : (s + 1) * node] = jnp.where(hit, 1.0, 0.0).astype(jnp.bfloat16)
        return 0

    loads[0].wait()
    lax.fori_loop(0, node // slab, build_faces, 0)
    for load in loads[1:4]:
        load.wait()
    lane = lax.broadcasted_iota(jnp.int32, (1, iface), 1)
    for t in range(2):
        for a in range(3):
            for b in range(3):
                weights[t, a, b] = jnp.where(lane < count_ref[t], couple_ref[a, b, t : t + 1, :], 0.0)

    for t in range(2):
        for it in range(2):

            @pl.when((dom == 0) if t == 0 else (sub == 0))
            def _():
                in_halo[it, 2 * t] = jnp.zeros((3 * width, iface), F32)

            @pl.when((dom == n_dom - 1) if t == 0 else (sub == n_sub - 1))
            def _():
                in_halo[it, 2 * t + 1] = jnp.zeros((3 * width, iface), F32)

    pl.semaphore_wait(barrier, n_all - 1)

    def col_copy(v):
        return pltpu.make_async_remote_copy(
            src_ref=basis.at[v, col], dst_ref=basis.at[v, col],
            send_sem=col_send.at[v], recv_sem=col_recv.at[v],
            device_id={"col": 1 - col}, device_id_type=MESH,
        )

    def halo_copy(it, slot):
        axis, here = ("dom", dom) if slot < 2 else ("sub", sub)
        step = 1 if slot % 2 == 0 else -1
        return pltpu.make_async_remote_copy(
            src_ref=out_halo.at[it, slot], dst_ref=in_halo.at[it, slot],
            send_sem=halo_send.at[it, slot], recv_sem=halo_recv.at[it, slot],
            device_id={axis: here + step}, device_id_type=MESH,
        )

    def sends(slot):
        here, count = (dom, n_dom) if slot < 2 else (sub, n_sub)
        return here < count - 1 if slot % 2 == 0 else here > 0

    def receives(slot):
        here, count = (dom, n_dom) if slot < 2 else (sub, n_sub)
        return here > 0 if slot % 2 == 0 else here < count - 1

    def part(value, a):
        return value[a * width : (a + 1) * width]

    def mix_up(t, value):
        return jnp.concatenate(
            [sum(weights[t, a, b] * part(value, a) for a in range(3)) for b in range(3)], axis=0
        )

    def mix_down(t, value):
        return jnp.concatenate(
            [sum(weights[t, a, b] * part(value, b) for b in range(3)) for a in range(3)], axis=0
        )

    def whole(v, a):
        return jnp.concatenate([basis[v, h, a] for h in range(n_col)], axis=0)

    def products(left, right):
        full = joined(sum(dot(left[a], right[a], NT) for a in range(3)))
        half = full.shape[1] // 2
        return full[:, :half] + full[:, half:]

    col_copy(0).start()

    for it in range(2):
        field = [basis[it, col, a] for a in range(3)]
        stacked = halves(jnp.concatenate(field, axis=0))
        for t in range(2):
            low = slice(inner + 2 * t * iface, inner + (2 * t + 1) * iface)
            high = slice(inner + (2 * t + 1) * iface, inner + (2 * t + 2) * iface)
            out_halo[it, 2 * t] = mix_up(t, joined(dot(stacked, pick[:, high], NN)))
            out_halo[it, 2 * t + 1] = joined(dot(stacked, pick[:, low], NN))
            for slot in (2 * t, 2 * t + 1):

                @pl.when(sends(slot))
                def _():
                    halo_copy(it, slot).start()

        if it == 0:
            for load in loads[4:]:
                load.wait()
            lax.fori_loop(0, node // slab, build_inner, 0)
        result = [(diag_ref[a] - SHIFT) * field[a] for a in range(3)]
        returned = jnp.zeros((6 * width, node), F32)
        for s in range(slots):
            span = slice(s * node, (s + 1) * node)
            near = joined(dot(stacked, pick[:, span], NN))
            back = []
            for b in range(3):
                back.append(sum(vals_ref[a, b, s] * field[a] for a in range(3)))
            returned = returned + dot(halves(jnp.concatenate(back, axis=0)), pick[:, span], NT)
            for a in range(3):
                result[a] = result[a] + sum(vals_ref[a, b, s] * part(near, b) for b in range(3))

        if it == 1:
            col_copy(0).wait_recv()
            col_copy(1).wait_recv()
            own = [halves(jnp.concatenate([basis[0, col, a], field[a]], axis=0)) for a in range(3)]
            both = [halves(jnp.concatenate([whole(0, a), whole(1, a)], axis=0)) for a in range(3)]
            early = products(own, both)

        for slot in range(4):

            @pl.when(receives(slot))
            def _():
                halo_copy(it, slot).wait_recv()

        for t in range(2):
            first = inner + 2 * t * iface
            arrived = jnp.concatenate([in_halo[it, 2 * t], mix_down(t, in_halo[it, 2 * t + 1])], axis=1)
            returned = returned + dot(halves(arrived), pick[:, first : first + 2 * iface], NT)
        returned = joined(returned)
        for a in range(3):
            result[a] = result[a] + part(returned, a)
            basis[it + 1, col, a] = result[a]
        col_copy(it + 1).start()

    last = products([halves(result[a]) for a in range(3)], both)
    message[...] = jnp.concatenate(
        [early[:width, :total], early[width:], last[:, total:], jnp.zeros((width, 128 - 4 * total), F32)], axis=1
    )

    stage[me] = message[...]
    every_peer(lambda k: gram_copy(k).start())
    every_peer(lambda k: gram_copy(k).wait_recv())
    grams = jnp.concatenate(
        [sum(stage[i * n_col + h] for i in range(n_dom * n_sub)) for h in range(n_col)], axis=0
    )

    s0 = grams[:, : 2 * total]
    s1 = grams[:, total : 3 * total]
    s2 = grams[:, 2 * total : 4 * total]
    norms = s0[:, :total]
    curvature = s1[:, :total] + SHIFT * norms
    big = jnp.concatenate([s0, s1], axis=0)
    stiff = SHIFT * big + jnp.concatenate([s1, s2], axis=0)
    eye = jnp.where(
        lax.broadcasted_iota(jnp.int32, (total, total), 0) == lax.broadcasted_iota(jnp.int32, (total, total), 1), 1.0, 0.0
    )
    alpha0 = eliminate(curvature, norms)
    norms_inverse = eliminate(norms, eye)
    start = eye - SHIFT * alpha0
    mixed = jnp.concatenate([start, -alpha0], axis=0)
    fresh = dot(mixed, dot(big, mixed, NN, HIGHEST), TN, HIGHEST)
    beta = dot(norms_inverse, fresh, NN, HIGHEST)
    direction = jnp.concatenate([start + beta, -alpha0], axis=0)
    curvature = dot(direction, dot(stiff, direction, NN, HIGHEST), TN, HIGHEST)
    alpha1 = eliminate(curvature, fresh)
    moved = dot(direction, alpha1, NN, HIGHEST)
    p_move, q_move = moved[:total], moved[total:]
    nothing = jnp.zeros((total, total), F32)
    sol_mix = jnp.concatenate([alpha0 + p_move, q_move, nothing], axis=0)
    res_mix = jnp.concatenate([start - SHIFT * p_move, -alpha0 - p_move - SHIFT * q_move, -q_move], axis=0)
    parts = halves(jnp.concatenate([sol_mix, res_mix], axis=1).T)
    final = jnp.concatenate([parts, parts], axis=1)

    col_copy(2).wait_recv()
    for a in range(3):
        every = halves(jnp.concatenate([whole(0, a), whole(1, a), whole(2, a)], axis=0))
        answer = joined(dot(final, every, NN))
        out_ref[0, a] = jnp.where(col == 0, answer[:width], answer[width:total])
        out_ref[1, a] = jnp.where(col == 0, answer[total : total + width], answer[total + width :])

    for v in range(3):
        col_copy(v).wait_send()
    for it in range(2):
        for slot in range(4):

            @pl.when(sends(slot))
            def _():
                halo_copy(it, slot).wait_send()

    every_peer(lambda k: gram_copy(k).wait_send())


def body(n_dom, n_sub, n_col, rhs, diagonal, lower_vals, lower_cols, face_nodes, couple, face_count):
    shape = rhs.shape[2:]
    _, width, node = shape
    slots = lower_cols.shape[2]
    iface = face_nodes.shape[3]
    vmem = pl.BlockSpec(memory_space=pltpu.VMEM)
    dma = pltpu.SemaphoreType.DMA
    out = pl.pallas_call(
        functools.partial(kernel, n_dom, n_sub, n_col),
        out_shape=jax.ShapeDtypeStruct((2, *shape), F32),
        in_specs=[pl.BlockSpec(memory_space=pltpu.HBM)] * 7,
        out_specs=vmem,
        scratch_shapes=[
            pltpu.VMEM((3, 1, node), F32),
            pltpu.VMEM((3, 3, slots, 1, node), F32),
            pltpu.VMEM((slots, 1, node), jnp.int32),
            pltpu.VMEM((4, iface), jnp.int32),
            pltpu.VMEM((3, 3, 2, iface), F32),
            pltpu.SMEM((2,), jnp.int32),
            dma((7,)),
            pltpu.VMEM((node, slots * node + 4 * iface), jnp.bfloat16),
            pltpu.VMEM((3, n_col, 3, width, node), F32),
            pltpu.VMEM((2, 4, 3 * width, iface), F32),
            pltpu.VMEM((2, 4, 3 * width, iface), F32),
            pltpu.VMEM((2, 3, 3, 1, iface), F32),
            pltpu.VMEM((width, 128), F32),
            pltpu.VMEM((n_dom * n_sub * n_col, width, 128), F32),
            dma((2, 4)),
            dma((2, 4)),
            dma((3,)),
            dma((3,)),
            dma((n_dom * n_sub * n_col,)),
            dma((n_dom * n_sub * n_col,)),
        ],
        compiler_params=pltpu.CompilerParams(
            collective_id=0, has_side_effects=True, vmem_limit_bytes=64 * 1024 * 1024
        ),
    )(
        rhs[0, 0], diagonal[0, 0][:, None], lower_vals[0, 0][:, :, :, None], lower_cols[0, 0][:, None],
        face_nodes[0, 0], jnp.transpose(couple[0, 0], (1, 2, 0, 3)), face_count[0, 0],
    )
    return out[0][None, None], out[1][None, None]


def solution(mesh):
    field = P(("groups", "dom"), "sub", None, "col", None)
    placed = (
        field,
        P("dom", "sub", None, None),
        P("dom", "sub", None, None, None, None),
        P("dom", "sub", None, None),
        P("dom", "sub", None, None),
        P("dom", "sub", None, None, None, None),
        P("dom", "sub", None),
    )
    return jax.shard_map(
        functools.partial(body, mesh.shape["dom"], mesh.shape["sub"], mesh.shape["col"]),
        mesh=mesh,
        in_specs=placed,
        out_specs=(field, field),
        check_vma=False,
    )
```

```python
import functools

import jax
import jax.numpy as jnp
from jax import lax
from jax.experimental import pallas as pl
from jax.experimental.pallas import tpu as pltpu
from jax.sharding import PartitionSpec as P

MESH = pl.DeviceIdType.MESH
SHIFT = 2.0
HIGHEST = lax.Precision.HIGHEST
F32 = jnp.float32


def dot(left, right, dims, precision=None):
    return lax.dot_general(left, right, (dims, ((), ())), precision=precision, preferred_element_type=F32)


NN = ((1,), (0,))
NT = ((1,), (1,))
TN = ((0,), (0,))


def halves(value):
    high = value.astype(jnp.bfloat16).astype(F32)
    return jnp.concatenate([high, value - high], axis=0).astype(jnp.bfloat16)


def joined(value):
    rows = value.shape[0] // 2
    return value[:rows] + value[rows:]


def eliminate(matrix, right):
    order = matrix.shape[0]
    lanes = right.shape[1]
    row = lax.broadcasted_iota(jnp.int32, (order, lanes), 0)
    columns = [jnp.broadcast_to(matrix[:, j : j + 1], (order, lanes)) for j in range(order)]
    scale = jnp.zeros((order, lanes), F32)
    for k in range(order):
        inverse = 1.0 / columns[k][k : k + 1, :]
        scale = jnp.where(row == k, inverse, scale)
        factor = jnp.where(row == k, 0.0, columns[k] * inverse)
        for j in range(k + 1, order):
            columns[j] = columns[j] - factor * columns[j][k : k + 1, :]
        right = right - factor * right[k : k + 1, :]
    return right * scale


def kernel(
    n_dom, n_sub, n_col,
    rhs_hbm, diag_hbm, vals_hbm, cols_hbm, faces_hbm, couple_hbm, count_hbm,
    out_ref,
    diag_ref, vals_ref, cols_ref, faces_ref, couple_ref, count_ref, load_sem,
    pick, basis, out_halo, in_halo, weights, message, stage,
    halo_send, halo_recv, col_send, col_recv, gram_send, gram_recv,
):
    dom = lax.axis_index("dom")
    sub = lax.axis_index("sub")
    col = lax.axis_index("col")
    width = rhs_hbm.shape[1]
    node = rhs_hbm.shape[2]
    slots = cols_hbm.shape[0]
    iface = faces_hbm.shape[1]
    inner = slots * node
    total = width * n_col
    n_all = n_dom * n_sub * n_col
    me = (dom * n_sub + sub) * n_col + col

    def place(k):
        peer = lax.rem(me + k, n_all)
        return {
            "dom": lax.div(peer, n_sub * n_col),
            "sub": lax.rem(lax.div(peer, n_col), n_sub),
            "col": lax.rem(peer, n_col),
        }

    def every_peer(act):
        if n_all <= 32:
            for k in range(1, n_all):
                act(k)
        else:
            lax.fori_loop(1, n_all, lambda k, _: (act(k), 0)[1], 0)

    def gram_copy(k):
        return pltpu.make_async_remote_copy(
            src_ref=message, dst_ref=stage.at[me], send_sem=gram_send.at[k], recv_sem=gram_recv.at[k],
            device_id=place(k), device_id_type=MESH,
        )

    loads = [
        pltpu.make_async_copy(source, target, load_sem.at[i])
        for i, (source, target) in enumerate(
            [
                (faces_hbm, faces_ref), (rhs_hbm, basis.at[0, col]), (couple_hbm, couple_ref), (count_hbm, count_ref),
                (cols_hbm, cols_ref), (vals_hbm, vals_ref), (diag_hbm, diag_ref),
            ]
        )
    ]
    for load in loads:
        load.start()

    barrier = pltpu.get_barrier_semaphore()
    every_peer(lambda k: pl.semaphore_signal(barrier, inc=1, device_id=place(k), device_id_type=MESH))

    slab = 32

    def build_faces(i, _):
        rows = pl.ds(pl.multiple_of(i * slab, slab), slab)
        ids = lax.broadcasted_iota(jnp.int32, (slab, iface), 0) + i * slab
        for f in range(4):
            hit = ids == faces_ref[f : f + 1, :]
            pick[rows, inner + f * iface : inner + (f + 1) * iface] = jnp.where(hit, 1.0, 0.0).astype(jnp.bfloat16)
        return 0

    def build_inner(i, _):
        rows = pl.ds(pl.multiple_of(i * slab, slab), slab)
        ids = lax.broadcasted_iota(jnp.int32, (slab, node), 0) + i * slab
        for s in range(slots):
            hit = ids == cols_ref[s]
            pick[rows, s * node : (s + 1) * node] = jnp.where(hit, 1.0, 0.0).astype(jnp.bfloat16)
        return 0

    loads[0].wait()
    lax.fori_loop(0, node // slab, build_faces, 0)
    for load in loads[1:4]:
        load.wait()
    lane = lax.broadcasted_iota(jnp.int32, (1, iface), 1)
    for t in range(2):
        for a in range(3):
            for b in range(3):
                weights[t, a, b] = jnp.where(lane < count_ref[t], couple_ref[a, b, t : t + 1, :], 0.0)

    for t in range(2):
        for it in range(2):

            @pl.when((dom == 0) if t == 0 else (sub == 0))
            def _():
                in_halo[it, 2 * t] = jnp.zeros((3 * width, iface), F32)

            @pl.when((dom == n_dom - 1) if t == 0 else (sub == n_sub - 1))
            def _():
                in_halo[it, 2 * t + 1] = jnp.zeros((3 * width, iface), F32)

    def col_copy(v):
        return pltpu.make_async_remote_copy(
            src_ref=basis.at[v, col], dst_ref=basis.at[v, col],
            send_sem=col_send.at[v], recv_sem=col_recv.at[v],
            device_id={"col": 1 - col}, device_id_type=MESH,
        )

    def halo_copy(it, slot):
        axis, here = ("dom", dom) if slot < 2 else ("sub", sub)
        step = 1 if slot % 2 == 0 else -1
        return pltpu.make_async_remote_copy(
            src_ref=out_halo.at[it, slot], dst_ref=in_halo.at[it, slot],
            send_sem=halo_send.at[it, slot], recv_sem=halo_recv.at[it, slot],
            device_id={axis: here + step}, device_id_type=MESH,
        )

    def sends(slot):
        here, count = (dom, n_dom) if slot < 2 else (sub, n_sub)
        return here < count - 1 if slot % 2 == 0 else here > 0

    def receives(slot):
        here, count = (dom, n_dom) if slot < 2 else (sub, n_sub)
        return here > 0 if slot % 2 == 0 else here < count - 1

    def part(value, a):
        return value[a * width : (a + 1) * width]

    def mix_up(t, value):
        return jnp.concatenate(
            [sum(weights[t, a, b] * part(value, a) for a in range(3)) for b in range(3)], axis=0
        )

    def mix_down(t, value):
        return jnp.concatenate(
            [sum(weights[t, a, b] * part(value, b) for b in range(3)) for a in range(3)], axis=0
        )

    def whole(v, a):
        return jnp.concatenate([basis[v, h, a] for h in range(n_col)], axis=0)

    def products(left, right):
        full = joined(sum(dot(left[a], right[a], NT) for a in range(3)))
        half = full.shape[1] // 2
        return full[:, :half] + full[:, half:]

    def launch(it, slots_sent):
        for slot in slots_sent:

            @pl.when(sends(slot))
            def _():
                halo_copy(it, slot).start()

    for it in range(2):
        field = [basis[it, col, a] for a in range(3)]
        stacked = halves(jnp.concatenate(field, axis=0))
        for t in range(2):
            low = slice(inner + 2 * t * iface, inner + (2 * t + 1) * iface)
            high = slice(inner + (2 * t + 1) * iface, inner + (2 * t + 2) * iface)
            out_halo[it, 2 * t] = mix_up(t, joined(dot(stacked, pick[:, high], NN)))
            out_halo[it, 2 * t + 1] = joined(dot(stacked, pick[:, low], NN))
            if it == 1:
                launch(it, (2 * t, 2 * t + 1))
        if it == 0:
            pl.semaphore_wait(barrier, n_all - 1)
            launch(it, range(4))
            col_copy(0).start()
        if it == 0:
            for load in loads[4:]:
                load.wait()
            lax.fori_loop(0, node // slab, build_inner, 0)
        result = [(diag_ref[a] - SHIFT) * field[a] for a in range(3)]
        returned = jnp.zeros((6 * width, node), F32)
        for s in range(slots):
            span = slice(s * node, (s + 1) * node)
            near = joined(dot(stacked, pick[:, span], NN))
            back = []
            for b in range(3):
                back.append(sum(vals_ref[a, b, s] * field[a] for a in range(3)))
            returned = returned + dot(halves(jnp.concatenate(back, axis=0)), pick[:, span], NT)
            for a in range(3):
                result[a] = result[a] + sum(vals_ref[a, b, s] * part(near, b) for b in range(3))

        if it == 1:
            col_copy(0).wait_recv()
            col_copy(1).wait_recv()
            own = [halves(jnp.concatenate([basis[0, col, a], field[a]], axis=0)) for a in range(3)]
            both = [halves(jnp.concatenate([whole(0, a), whole(1, a)], axis=0)) for a in range(3)]
            early = products(own, both)

        for slot in range(4):

            @pl.when(receives(slot))
            def _():
                halo_copy(it, slot).wait_recv()

        for t in range(2):
            first = inner + 2 * t * iface
            arrived = jnp.concatenate([in_halo[it, 2 * t], mix_down(t, in_halo[it, 2 * t + 1])], axis=1)
            returned = returned + dot(halves(arrived), pick[:, first : first + 2 * iface], NT)
        returned = joined(returned)
        for a in range(3):
            result[a] = result[a] + part(returned, a)
            basis[it + 1, col, a] = result[a]
        col_copy(it + 1).start()

    last = products([halves(result[a]) for a in range(3)], both)
    message[...] = jnp.concatenate(
        [early[:width, :total], early[width:], last[:, total:], jnp.zeros((width, 128 - 4 * total), F32)], axis=1
    )

    stage[me] = message[...]
    every_peer(lambda k: gram_copy(k).start())
    every_peer(lambda k: gram_copy(k).wait_recv())
    grams = jnp.concatenate(
        [sum(stage[i * n_col + h] for i in range(n_dom * n_sub)) for h in range(n_col)], axis=0
    )

    s0 = grams[:, : 2 * total]
    s1 = grams[:, total : 3 * total]
    s2 = grams[:, 2 * total : 4 * total]
    norms = s0[:, :total]
    curvature = s1[:, :total] + SHIFT * norms
    big = jnp.concatenate([s0, s1], axis=0)
    stiff = SHIFT * big + jnp.concatenate([s1, s2], axis=0)
    eye = jnp.where(
        lax.broadcasted_iota(jnp.int32, (total, total), 0) == lax.broadcasted_iota(jnp.int32, (total, total), 1), 1.0, 0.0
    )
    alpha0 = eliminate(curvature, norms)
    norms_inverse = eliminate(norms, eye)
    start = eye - SHIFT * alpha0
    mixed = jnp.concatenate([start, -alpha0], axis=0)
    fresh = dot(mixed, dot(big, mixed, NN, HIGHEST), TN, HIGHEST)
    beta = dot(norms_inverse, fresh, NN, HIGHEST)
    direction = jnp.concatenate([start + beta, -alpha0], axis=0)
    curvature = dot(direction, dot(stiff, direction, NN, HIGHEST), TN, HIGHEST)
    alpha1 = eliminate(curvature, fresh)
    moved = dot(direction, alpha1, NN, HIGHEST)
    p_move, q_move = moved[:total], moved[total:]
    nothing = jnp.zeros((total, total), F32)
    sol_mix = jnp.concatenate([alpha0 + p_move, q_move, nothing], axis=0)
    res_mix = jnp.concatenate([start - SHIFT * p_move, -alpha0 - p_move - SHIFT * q_move, -q_move], axis=0)
    parts = halves(jnp.concatenate([sol_mix, res_mix], axis=1).T)
    final = jnp.concatenate([parts, parts], axis=1)

    col_copy(2).wait_recv()
    for a in range(3):
        every = halves(jnp.concatenate([whole(0, a), whole(1, a), whole(2, a)], axis=0))
        answer = joined(dot(final, every, NN))
        out_ref[0, a] = jnp.where(col == 0, answer[:width], answer[width:total])
        out_ref[1, a] = jnp.where(col == 0, answer[total : total + width], answer[total + width :])

    for v in range(3):
        col_copy(v).wait_send()
    for it in range(2):
        for slot in range(4):

            @pl.when(sends(slot))
            def _():
                halo_copy(it, slot).wait_send()

    every_peer(lambda k: gram_copy(k).wait_send())


def body(n_dom, n_sub, n_col, rhs, diagonal, lower_vals, lower_cols, face_nodes, couple, face_count):
    shape = rhs.shape[2:]
    _, width, node = shape
    slots = lower_cols.shape[2]
    iface = face_nodes.shape[3]
    vmem = pl.BlockSpec(memory_space=pltpu.VMEM)
    dma = pltpu.SemaphoreType.DMA
    out = pl.pallas_call(
        functools.partial(kernel, n_dom, n_sub, n_col),
        out_shape=jax.ShapeDtypeStruct((2, *shape), F32),
        in_specs=[pl.BlockSpec(memory_space=pltpu.HBM)] * 7,
        out_specs=vmem,
        scratch_shapes=[
            pltpu.VMEM((3, 1, node), F32),
            pltpu.VMEM((3, 3, slots, 1, node), F32),
            pltpu.VMEM((slots, 1, node), jnp.int32),
            pltpu.VMEM((4, iface), jnp.int32),
            pltpu.VMEM((3, 3, 2, iface), F32),
            pltpu.SMEM((2,), jnp.int32),
            dma((7,)),
            pltpu.VMEM((node, slots * node + 4 * iface), jnp.bfloat16),
            pltpu.VMEM((3, n_col, 3, width, node), F32),
            pltpu.VMEM((2, 4, 3 * width, iface), F32),
            pltpu.VMEM((2, 4, 3 * width, iface), F32),
            pltpu.VMEM((2, 3, 3, 1, iface), F32),
            pltpu.VMEM((width, 128), F32),
            pltpu.VMEM((n_dom * n_sub * n_col, width, 128), F32),
            dma((2, 4)),
            dma((2, 4)),
            dma((3,)),
            dma((3,)),
            dma((n_dom * n_sub * n_col,)),
            dma((n_dom * n_sub * n_col,)),
        ],
        compiler_params=pltpu.CompilerParams(
            collective_id=0, has_side_effects=True, vmem_limit_bytes=64 * 1024 * 1024
        ),
    )(
        rhs[0, 0], diagonal[0, 0][:, None], lower_vals[0, 0][:, :, :, None], lower_cols[0, 0][:, None],
        face_nodes[0, 0], jnp.transpose(couple[0, 0], (1, 2, 0, 3)), face_count[0, 0],
    )
    return out[0][None, None], out[1][None, None]


def solution(mesh):
    field = P(("groups", "dom"), "sub", None, "col", None)
    placed = (
        field,
        P("dom", "sub", None, None),
        P("dom", "sub", None, None, None, None),
        P("dom", "sub", None, None),
        P("dom", "sub", None, None),
        P("dom", "sub", None, None, None, None),
        P("dom", "sub", None),
    )
    return jax.shard_map(
        functools.partial(body, mesh.shape["dom"], mesh.shape["sub"], mesh.shape["col"]),
        mesh=mesh,
        in_specs=placed,
        out_specs=(field, field),
        check_vma=False,
    )
```

```python
import functools

import jax
import jax.numpy as jnp
from jax import lax
from jax.experimental import pallas as pl
from jax.experimental.pallas import tpu as pltpu
from jax.sharding import PartitionSpec as P

MESH = pl.DeviceIdType.MESH
SHIFT = 2.0
HIGHEST = lax.Precision.HIGHEST
F32 = jnp.float32


def dot(left, right, dims, precision=None):
    return lax.dot_general(left, right, (dims, ((), ())), precision=precision, preferred_element_type=F32)


NN = ((1,), (0,))
NT = ((1,), (1,))
TN = ((0,), (0,))


def halves(value):
    high = value.astype(jnp.bfloat16).astype(F32)
    return jnp.concatenate([high, value - high], axis=0).astype(jnp.bfloat16)


def joined(value):
    rows = value.shape[0] // 2
    return value[:rows] + value[rows:]


def eliminate(matrix, right):
    order = matrix.shape[0]
    lanes = right.shape[1]
    row = lax.broadcasted_iota(jnp.int32, (order, lanes), 0)
    columns = [jnp.broadcast_to(matrix[:, j : j + 1], (order, lanes)) for j in range(order)]
    scale = jnp.zeros((order, lanes), F32)
    for k in range(order):
        inverse = 1.0 / columns[k][k : k + 1, :]
        scale = jnp.where(row == k, inverse, scale)
        factor = jnp.where(row == k, 0.0, columns[k] * inverse)
        for j in range(k + 1, order):
            columns[j] = columns[j] - factor * columns[j][k : k + 1, :]
        right = right - factor * right[k : k + 1, :]
    return right * scale


def kernel(
    n_dom, n_sub, n_col,
    rhs_hbm, diag_hbm, vals_hbm, cols_hbm, faces_hbm, couple_hbm, count_hbm,
    out_ref,
    diag_ref, vals_ref, cols_ref, faces_ref, couple_ref, count_ref, load_sem,
    pick, basis, out_halo, in_halo, weights, message, stage,
    halo_send, halo_recv, col_send, col_recv, gram_send, gram_recv, pair_sem,
):
    dom = lax.axis_index("dom")
    sub = lax.axis_index("sub")
    col = lax.axis_index("col")
    width = rhs_hbm.shape[1]
    node = rhs_hbm.shape[2]
    slots = cols_hbm.shape[0]
    iface = faces_hbm.shape[1]
    inner = slots * node
    total = width * n_col
    n_all = n_dom * n_sub
    me = dom * n_sub + sub

    def place(k):
        peer = lax.rem(me + k, n_all)
        return {"dom": lax.div(peer, n_sub), "sub": lax.rem(peer, n_sub)}

    def every_peer(act):
        if n_all <= 32:
            for k in range(1, n_all):
                act(k)
        else:
            lax.fori_loop(1, n_all, lambda k, _: (act(k), 0)[1], 0)

    def gram_copy(k):
        return pltpu.make_async_remote_copy(
            src_ref=message, dst_ref=stage.at[me], send_sem=gram_send.at[k], recv_sem=gram_recv.at[k],
            device_id=place(k), device_id_type=MESH,
        )

    loads = [
        pltpu.make_async_copy(source, target, load_sem.at[i])
        for i, (source, target) in enumerate(
            [
                (faces_hbm, faces_ref), (rhs_hbm, basis.at[0, col]), (couple_hbm, couple_ref), (count_hbm, count_ref),
                (cols_hbm, cols_ref), (vals_hbm, vals_ref), (diag_hbm, diag_ref),
            ]
        )
    ]
    for load in loads:
        load.start()

    pair_copy = pltpu.make_async_remote_copy(
        src_ref=message.at[col], dst_ref=message.at[col], send_sem=pair_sem.at[0], recv_sem=pair_sem.at[1],
        device_id={"col": 1 - col}, device_id_type=MESH,
    )

    barrier = pltpu.get_barrier_semaphore()
    pl.semaphore_signal(barrier, inc=1, device_id={"col": 1 - col}, device_id_type=MESH)
    every_peer(lambda k: pl.semaphore_signal(barrier, inc=1, device_id=place(k), device_id_type=MESH))

    slab = 32

    def build_faces(i, _):
        rows = pl.ds(pl.multiple_of(i * slab, slab), slab)
        ids = lax.broadcasted_iota(jnp.int32, (slab, iface), 0) + i * slab
        for f in range(4):
            hit = ids == faces_ref[f : f + 1, :]
            pick[rows, inner + f * iface : inner + (f + 1) * iface] = jnp.where(hit, 1.0, 0.0).astype(jnp.bfloat16)
        return 0

    def build_inner(i, _):
        rows = pl.ds(pl.multiple_of(i * slab, slab), slab)
        ids = lax.broadcasted_iota(jnp.int32, (slab, node), 0) + i * slab
        for s in range(slots):
            hit = ids == cols_ref[s]
            pick[rows, s * node : (s + 1) * node] = jnp.where(hit, 1.0, 0.0).astype(jnp.bfloat16)
        return 0

    loads[0].wait()
    lax.fori_loop(0, node // slab, build_faces, 0)
    for load in loads[1:4]:
        load.wait()
    lane = lax.broadcasted_iota(jnp.int32, (1, iface), 1)
    for t in range(2):
        for a in range(3):
            for b in range(3):
                weights[t, a, b] = jnp.where(lane < count_ref[t], couple_ref[a, b, t : t + 1, :], 0.0)

    for t in range(2):
        for it in range(2):

            @pl.when((dom == 0) if t == 0 else (sub == 0))
            def _():
                in_halo[it, 2 * t] = jnp.zeros((3 * width, iface), F32)

            @pl.when((dom == n_dom - 1) if t == 0 else (sub == n_sub - 1))
            def _():
                in_halo[it, 2 * t + 1] = jnp.zeros((3 * width, iface), F32)

    def col_copy(v):
        return pltpu.make_async_remote_copy(
            src_ref=basis.at[v, col], dst_ref=basis.at[v, col],
            send_sem=col_send.at[v], recv_sem=col_recv.at[v],
            device_id={"col": 1 - col}, device_id_type=MESH,
        )

    def halo_copy(it, slot):
        axis, here = ("dom", dom) if slot < 2 else ("sub", sub)
        step = 1 if slot % 2 == 0 else -1
        return pltpu.make_async_remote_copy(
            src_ref=out_halo.at[it, slot], dst_ref=in_halo.at[it, slot],
            send_sem=halo_send.at[it, slot], recv_sem=halo_recv.at[it, slot],
            device_id={axis: here + step}, device_id_type=MESH,
        )

    def sends(slot):
        here, count = (dom, n_dom) if slot < 2 else (sub, n_sub)
        return here < count - 1 if slot % 2 == 0 else here > 0

    def receives(slot):
        here, count = (dom, n_dom) if slot < 2 else (sub, n_sub)
        return here > 0 if slot % 2 == 0 else here < count - 1

    def part(value, a):
        return value[a * width : (a + 1) * width]

    def mix_up(t, value):
        return jnp.concatenate(
            [sum(weights[t, a, b] * part(value, a) for a in range(3)) for b in range(3)], axis=0
        )

    def mix_down(t, value):
        return jnp.concatenate(
            [sum(weights[t, a, b] * part(value, b) for b in range(3)) for a in range(3)], axis=0
        )

    def whole(v, a):
        return jnp.concatenate([basis[v, h, a] for h in range(n_col)], axis=0)

    def products(left, right):
        full = joined(sum(dot(left[a], right[a], NT) for a in range(3)))
        half = full.shape[1] // 2
        return full[:, :half] + full[:, half:]

    def launch(it, slots_sent):
        for slot in slots_sent:

            @pl.when(sends(slot))
            def _():
                halo_copy(it, slot).start()

    for it in range(2):
        field = [basis[it, col, a] for a in range(3)]
        stacked = halves(jnp.concatenate(field, axis=0))
        for t in range(2):
            low = slice(inner + 2 * t * iface, inner + (2 * t + 1) * iface)
            high = slice(inner + (2 * t + 1) * iface, inner + (2 * t + 2) * iface)
            out_halo[it, 2 * t] = mix_up(t, joined(dot(stacked, pick[:, high], NN)))
            out_halo[it, 2 * t + 1] = joined(dot(stacked, pick[:, low], NN))
            if it == 1:
                launch(it, (2 * t, 2 * t + 1))
        if it == 0:
            pl.semaphore_wait(barrier, n_all)
            launch(it, range(4))
            col_copy(0).start()
        if it == 0:
            for load in loads[4:]:
                load.wait()
            lax.fori_loop(0, node // slab, build_inner, 0)
        result = [(diag_ref[a] - SHIFT) * field[a] for a in range(3)]
        returned = jnp.zeros((6 * width, node), F32)
        for s in range(slots):
            span = slice(s * node, (s + 1) * node)
            near = joined(dot(stacked, pick[:, span], NN))
            back = []
            for b in range(3):
                back.append(sum(vals_ref[a, b, s] * field[a] for a in range(3)))
            returned = returned + dot(halves(jnp.concatenate(back, axis=0)), pick[:, span], NT)
            for a in range(3):
                result[a] = result[a] + sum(vals_ref[a, b, s] * part(near, b) for b in range(3))

        if it == 1:
            col_copy(0).wait_recv()
            col_copy(1).wait_recv()
            own = [halves(jnp.concatenate([basis[0, col, a], field[a]], axis=0)) for a in range(3)]
            both = [halves(jnp.concatenate([whole(0, a), whole(1, a)], axis=0)) for a in range(3)]
            early = products(own, both)

        for slot in range(4):

            @pl.when(receives(slot))
            def _():
                halo_copy(it, slot).wait_recv()

        for t in range(2):
            first = inner + 2 * t * iface
            arrived = jnp.concatenate([in_halo[it, 2 * t], mix_down(t, in_halo[it, 2 * t + 1])], axis=1)
            returned = returned + dot(halves(arrived), pick[:, first : first + 2 * iface], NT)
        returned = joined(returned)
        for a in range(3):
            result[a] = result[a] + part(returned, a)
            basis[it + 1, col, a] = result[a]
        if it == 0:
            col_copy(1).start()

    last = products([halves(result[a]) for a in range(3)], both)
    message[col] = jnp.concatenate(
        [early[:width, :total], early[width:], last[:, total:], jnp.zeros((width, 128 - 4 * total), F32)], axis=1
    )

    pair_copy.start()
    col_copy(2).start()
    pair_copy.wait_recv()
    every_peer(lambda k: gram_copy(k).start())
    stage[me] = message[...]
    every_peer(lambda k: gram_copy(k).wait_recv())
    grams = jnp.concatenate(
        [sum(stage[i, h] for i in range(n_all)) for h in range(n_col)], axis=0
    )

    s0 = grams[:, : 2 * total]
    s1 = grams[:, total : 3 * total]
    s2 = grams[:, 2 * total : 4 * total]
    norms = s0[:, :total]
    curvature = s1[:, :total] + SHIFT * norms
    big = jnp.concatenate([s0, s1], axis=0)
    stiff = SHIFT * big + jnp.concatenate([s1, s2], axis=0)
    eye = jnp.where(
        lax.broadcasted_iota(jnp.int32, (total, total), 0) == lax.broadcasted_iota(jnp.int32, (total, total), 1), 1.0, 0.0
    )
    alpha0 = eliminate(curvature, norms)
    norms_inverse = eliminate(norms, eye)
    start = eye - SHIFT * alpha0
    mixed = jnp.concatenate([start, -alpha0], axis=0)
    fresh = dot(mixed, dot(big, mixed, NN, HIGHEST), TN, HIGHEST)
    beta = dot(norms_inverse, fresh, NN, HIGHEST)
    direction = jnp.concatenate([start + beta, -alpha0], axis=0)
    curvature = dot(direction, dot(stiff, direction, NN, HIGHEST), TN, HIGHEST)
    alpha1 = eliminate(curvature, fresh)
    moved = dot(direction, alpha1, NN, HIGHEST)
    p_move, q_move = moved[:total], moved[total:]
    nothing = jnp.zeros((total, total), F32)
    sol_mix = jnp.concatenate([alpha0 + p_move, q_move, nothing], axis=0)
    res_mix = jnp.concatenate([start - SHIFT * p_move, -alpha0 - p_move - SHIFT * q_move, -q_move], axis=0)
    parts = halves(jnp.concatenate([sol_mix, res_mix], axis=1).T)
    final = jnp.concatenate([parts, parts], axis=1)

    col_copy(2).wait_recv()
    for a in range(3):
        every = halves(jnp.concatenate([whole(0, a), whole(1, a), whole(2, a)], axis=0))
        answer = joined(dot(final, every, NN))
        out_ref[0, a] = jnp.where(col == 0, answer[:width], answer[width:total])
        out_ref[1, a] = jnp.where(col == 0, answer[total : total + width], answer[total + width :])

    for v in range(3):
        col_copy(v).wait_send()
    for it in range(2):
        for slot in range(4):

            @pl.when(sends(slot))
            def _():
                halo_copy(it, slot).wait_send()

    pair_copy.wait_send()
    every_peer(lambda k: gram_copy(k).wait_send())


def body(n_dom, n_sub, n_col, rhs, diagonal, lower_vals, lower_cols, face_nodes, couple, face_count):
    shape = rhs.shape[2:]
    _, width, node = shape
    slots = lower_cols.shape[2]
    iface = face_nodes.shape[3]
    vmem = pl.BlockSpec(memory_space=pltpu.VMEM)
    dma = pltpu.SemaphoreType.DMA
    out = pl.pallas_call(
        functools.partial(kernel, n_dom, n_sub, n_col),
        out_shape=jax.ShapeDtypeStruct((2, *shape), F32),
        in_specs=[pl.BlockSpec(memory_space=pltpu.HBM)] * 7,
        out_specs=vmem,
        scratch_shapes=[
            pltpu.VMEM((3, 1, node), F32),
            pltpu.VMEM((3, 3, slots, 1, node), F32),
            pltpu.VMEM((slots, 1, node), jnp.int32),
            pltpu.VMEM((4, iface), jnp.int32),
            pltpu.VMEM((3, 3, 2, iface), F32),
            pltpu.SMEM((2,), jnp.int32),
            dma((7,)),
            pltpu.VMEM((node, slots * node + 4 * iface), jnp.bfloat16),
            pltpu.VMEM((3, n_col, 3, width, node), F32),
            pltpu.VMEM((2, 4, 3 * width, iface), F32),
            pltpu.VMEM((2, 4, 3 * width, iface), F32),
            pltpu.VMEM((2, 3, 3, 1, iface), F32),
            pltpu.VMEM((n_col, width, 128), F32),
            pltpu.VMEM((n_dom * n_sub, n_col, width, 128), F32),
            dma((2, 4)),
            dma((2, 4)),
            dma((3,)),
            dma((3,)),
            dma((n_dom * n_sub,)),
            dma((n_dom * n_sub,)),
            dma((2,)),
        ],
        compiler_params=pltpu.CompilerParams(
            collective_id=0, has_side_effects=True, vmem_limit_bytes=64 * 1024 * 1024
        ),
    )(
        rhs[0, 0], diagonal[0, 0][:, None], lower_vals[0, 0][:, :, :, None], lower_cols[0, 0][:, None],
        face_nodes[0, 0], jnp.transpose(couple[0, 0], (1, 2, 0, 3)), face_count[0, 0],
    )
    return out[0][None, None], out[1][None, None]


def solution(mesh):
    field = P(("groups", "dom"), "sub", None, "col", None)
    placed = (
        field,
        P("dom", "sub", None, None),
        P("dom", "sub", None, None, None, None),
        P("dom", "sub", None, None),
        P("dom", "sub", None, None),
        P("dom", "sub", None, None, None, None),
        P("dom", "sub", None),
    )
    return jax.shard_map(
        functools.partial(body, mesh.shape["dom"], mesh.shape["sub"], mesh.shape["col"]),
        mesh=mesh,
        in_specs=placed,
        out_specs=(field, field),
        check_vma=False,
    )
```
